32 devices in a mesh: rep: 8 (over y, x, core), shard: 4 (over z).
Axes of the slice: x: 2, y: 2, z: 4, core: 2. Of those that a mesh axis runs over, the one named last changes fastest.
Arguments:
- activations: bfloat16 [4096, 4096], P(('rep', 'shard')), may hold values from -6 to 6
- cotangent: bfloat16 [4096, 896], P(('rep', 'shard')), may hold values from -0.099609375 to 0.099609375
- weight: bfloat16 [8, 4096, 896], P('rep', 'shard'), may hold values from -6 to 6
- momentum: bfloat16 [8, 4096, 896], P('rep', 'shard'), may hold values from -6 to 6
- step_index: int32 [1], replicated, may hold values from 0 to 999
Outputs:
- averaged: bfloat16 [8, 4096, 896], P('rep', 'shard')
- momentum_new: bfloat16 [8, 4096, 896], P('rep', 'shard')
The draws below stay inside these ranges and needn't reach their ends.
All inputs are finite; a program needn't handle non-finite values.
Results may differ from the reference program's by a relative error of at most 0.012.
Values may be sent and summed in bfloat16 or wider, within the bound.
A program may use at most 64 MiB of HBM per device.

```python
import jax
import jax.numpy as jnp
from jax import lax

D = 4096
HID = 448
TOK_DEV = 128
TOKENS = 4096
N_REP = 8
N_SHARD = 4


def raised(drawn, rng, source, target, shards_of, factor):
    def block_of(position):
        return (jnp.arange(drawn.shape[position]) // (drawn.shape[position] // shards_of)).reshape((-1,) + (1,) * (drawn.ndim - 1 - position))

    near = jax.random.permutation(rng, shards_of)[block_of(target)]
    far = (block_of(target) + shards_of // 2) % shards_of
    return jnp.where((block_of(source) == near) | (block_of(source) == far), factor * drawn, drawn)


def block_levels(own_key, shape, split, low, largest):
    loudness, own = 1.0, jax.random.fold_in(own_key, 6)
    for position, shards_of in split:
        steps = jnp.exp(jax.random.uniform(jax.random.fold_in(own, position), (shards_of,), jnp.float32, low / len(split), largest / len(split)))
        loudness = loudness * jnp.repeat(steps, shape[position] // shards_of).reshape([-1 if axis == position else 1 for axis in range(len(shape))])
    return loudness


def normal_values(stream_key, shape, spread, bound, shards=(), held_as=jnp.bfloat16):
    loudness = block_levels(stream_key, shape, shards, -0.22, 0.18) if shards else 1.0
    drawn = jax.random.normal(stream_key, shape, jnp.float32) * spread * loudness
    return jnp.minimum(jnp.maximum(drawn, -bound), bound).astype(held_as)


def bell_draw_with(stream_key, dims, width, bound, cuts, heavy, kind=jnp.bfloat16):
    array = width * jax.random.normal(stream_key, dims, jnp.float32)
    if cuts:
        array = array * block_levels(stream_key, dims, cuts, -0.22, 0.18)
    return jnp.clip(raised(array, jax.random.fold_in(stream_key, 3), *heavy), -bound, bound).astype(kind)


def setup_inputs(seed: int = 0) -> dict:
    key_of = jax.random.split(jax.random.key(seed), 6)
    return {
        "activations": bell_draw_with(key_of[0], (TOKENS, D), 1.0, 6.0, ((0, 32),), (0, 1, 32, 2.75)),
        "cotangent": normal_values(key_of[1], (TOKENS, 2 * HID), 0.015625, 0.099609375, ((0, 32),)),
        "weight": normal_values(key_of[2], (N_REP, D, 2 * HID), 1.0, 6.0, ((0, 8), (1, 4))),
        "momentum": normal_values(key_of[3], (N_REP, D, 2 * HID), 1.0, 6.0, ((0, 8), (1, 4))),
        "step_index": jax.random.randint(key_of[4], (1,), 0, 1000).astype(jnp.int32),
    }


def replica_gradient(paired):
    blocks_rows = paired[0].reshape(N_SHARD, TOK_DEV, D)
    blocks_cot = paired[1].reshape(N_SHARD, TOK_DEV, 2 * HID)

    def add_block(total, pair):
        part = jnp.dot(pair[0].T, pair[1], preferred_element_type=jnp.float32)
        rounded = lax.optimization_barrier(part.astype(jnp.bfloat16)).astype(jnp.float32)
        return total + rounded, None

    start = jnp.zeros((D, 2 * HID), jnp.float32)
    total, unused = lax.scan(add_block, start, (blocks_rows, blocks_cot))
    return total


def reference(activations, cotangent, weight, momentum, step_index):
    levels = N_REP.bit_length() - 1
    grouped_rows = activations.reshape(N_REP, N_SHARD * TOK_DEV, D)
    grouped_cot = cotangent.reshape(N_REP, N_SHARD * TOK_DEV, 2 * HID)
    gradient = lax.map(replica_gradient, (grouped_rows, grouped_cot))
    momentum_new = (0.9 * momentum.astype(jnp.float32) + gradient).astype(jnp.bfloat16)
    half_step = (weight.astype(jnp.float32) - 0.5 * momentum_new.astype(jnp.float32)).astype(jnp.bfloat16)
    distance = jnp.left_shift(jnp.int32(1), (step_index[0] % levels).astype(jnp.int32))
    source = ((jnp.arange(N_REP, dtype=jnp.int32) - distance) % N_REP).astype(jnp.int32)
    received = jnp.take(half_step, source, axis=0)
    averaged = (0.5 * (half_step.astype(jnp.float32) + received.astype(jnp.float32))).astype(jnp.bfloat16)
    return averaged, momentum_new
```

```python
import functools

import jax
import jax.numpy as jnp
from jax import lax
from jax.experimental import pallas as pl
from jax.experimental.pallas import tpu as pltpu
from jax.sharding import PartitionSpec as P

MESH = pl.DeviceIdType.MESH
STEP = 128


def cuts(size, step):
    step = step if size % step == 0 else size
    return [(at, step) for at in range(0, size, step)]


def plan(rows, cols):
    a_chunks, c_chunks = cuts(rows, STEP), cuts(cols, STEP)
    order = sorted(
        [((i + 1) / len(c_chunks), 0, "c", i) for i in range(len(c_chunks))]
        + [((i + 1) / len(a_chunks), 1, "a", i) for i in range(len(a_chunks))]
    )
    events, rows_in, cols_in = [], 0, 0
    for _, _, kind, i in order:
        if kind == "a":
            at, size = a_chunks[i]
            block = (at, size, 0, cols_in)
            rows_in = at + size
        else:
            at, size = c_chunks[i]
            block = (0, rows_in, at, size)
            cols_in = at + size
        events.append((kind, i, at, size, block if block[1] and block[3] else None))
    return events


def kernel(
    n_rep,
    n_shard,
    by,
    act,
    cot,
    weight,
    momentum,
    avg_out,
    mom_out,
    act_all,
    cot_all,
    w_in,
    m_in,
    m_new,
    half,
    other,
    avg,
    load_sem,
    act_send,
    act_recv,
    cot_send,
    cot_recv,
    rep_send,
    rep_recv,
    mom_sem,
    avg_sem,
):
    rep, shard = lax.axis_index("rep"), lax.axis_index("shard")
    tok = cot.shape[0]
    rows, cols = weight.shape
    events = plan(rows, cols)
    ahead = lax.rem(rep + by, n_rep)
    behind = lax.rem(rep + (n_rep - by), n_rep)

    mine = pl.ds(pl.multiple_of(shard * tok, tok), tok)
    loads = [
        pltpu.make_async_copy(
            act.at[:, pl.ds(pl.multiple_of(shard * rows, rows), rows)], act_all.at[mine, :], load_sem.at[0]
        ),
        pltpu.make_async_copy(cot, cot_all.at[mine, :], load_sem.at[1]),
        pltpu.make_async_copy(momentum, m_in, load_sem.at[2]),
        pltpu.make_async_copy(weight, w_in, load_sem.at[3]),
    ]
    for load in loads:
        load.start()

    barrier = pltpu.get_barrier_semaphore()
    for off in range(1, n_shard):
        pl.semaphore_signal(
            barrier, inc=1, device_id={"shard": lax.rem(shard + off, n_shard)}, device_id_type=MESH
        )
    for partner in (ahead, behind):
        pl.semaphore_signal(barrier, inc=1, device_id={"rep": partner}, device_id_type=MESH)
    pl.semaphore_wait(barrier, n_shard + 1)

    sends = {}
    for kind, i, at, size, _ in events:
        for off in range(1, n_shard):
            to = lax.rem(shard + off, n_shard)
            if kind == "a":
                copy = pltpu.make_async_remote_copy(
                    src_ref=act.at[:, pl.ds(pl.multiple_of(to * rows + at, size), size)],
                    dst_ref=act_all.at[mine, pl.ds(at, size)],
                    send_sem=act_send.at[i, off - 1],
                    recv_sem=act_recv.at[i, off - 1],
                    device_id={"shard": to},
                    device_id_type=MESH,
                )
            else:
                copy = pltpu.make_async_remote_copy(
                    src_ref=cot.at[:, pl.ds(at, size)],
                    dst_ref=cot_all.at[mine, pl.ds(at, size)],
                    send_sem=cot_send.at[i, off - 1],
                    recv_sem=cot_recv.at[i, off - 1],
                    device_id={"shard": to},
                    device_id_type=MESH,
                )
            copy.start()
            sends[kind, i, off] = copy

    for load in loads:
        load.wait()

    tile = STEP if rows % STEP == 0 else rows
    outs, reps, blocks = [], [], []
    for kind, i, at, size, block in events:
        for off in range(1, n_shard):
            sends[kind, i, off].wait_recv()
        if block is None:
            continue
        r0, height, c0, width = block
        across = pl.ds(c0, width)

        def one(t, _):
            down = pl.ds(pl.multiple_of(r0 + t * tile, tile), tile)
            grad = lax.dot_general(
                act_all[:, down],
                cot_all[:, across],
                (((0,), (0,)), ((), ())),
                preferred_element_type=jnp.float32,
            )
            new = (0.9 * m_in[down, across].astype(jnp.float32) + grad).astype(jnp.bfloat16)
            m_new[down, across] = new
            half[down, across] = (
                w_in[down, across].astype(jnp.float32) - 0.5 * new.astype(jnp.float32)
            ).astype(jnp.bfloat16)
            return 0

        lax.fori_loop(0, height // tile, one, 0)
        e = len(blocks)
        here = (pl.ds(r0, height), across)
        copy = pltpu.make_async_remote_copy(
            src_ref=half.at[here],
            dst_ref=other.at[here],
            send_sem=rep_send.at[e],
            recv_sem=rep_recv.at[e],
            device_id={"rep": ahead},
            device_id_type=MESH,
        )
        copy.start()
        reps.append(copy)
        out = pltpu.make_async_copy(m_new.at[here], mom_out.at[here], mom_sem.at[e])
        out.start()
        outs.append(out)
        blocks.append(block)

    for e, (r0, height, c0, width) in enumerate(blocks):
        reps[e].wait_recv()
        across = pl.ds(c0, width)

        def mean(t, _):
            down = pl.ds(pl.multiple_of(r0 + t * tile, tile), tile)
            avg[down, across] = (
                0.5 * (half[down, across].astype(jnp.float32) + other[down, across].astype(jnp.float32))
            ).astype(jnp.bfloat16)
            return 0

        lax.fori_loop(0, height // tile, mean, 0)
        here = (pl.ds(r0, height), across)
        out = pltpu.make_async_copy(avg.at[here], avg_out.at[here], avg_sem.at[e])
        out.start()
        outs.append(out)

    for copy in sends.values():
        copy.wait_send()
    for copy in reps:
        copy.wait_send()
    for out in outs:
        out.wait()


def fused(n_rep, n_shard, level, activations, cotangent, weight, momentum):
    tok, (rows, cols) = cotangent.shape[0], weight.shape
    events = plan(rows, cols)
    n_a = sum(kind == "a" for kind, *_ in events)
    n_c = len(events) - n_a
    n_b = sum(event[-1] is not None for event in events)
    dma = pltpu.SemaphoreType.DMA
    whole = pltpu.VMEM((rows, cols), jnp.bfloat16)
    shape = jax.ShapeDtypeStruct((rows, cols), jnp.bfloat16)
    anywhere = pl.BlockSpec(memory_space=pl.ANY)
    return pl.pallas_call(
        functools.partial(kernel, n_rep, n_shard, 1 << level),
        out_shape=(shape, shape),
        in_specs=[anywhere] * 4,
        out_specs=(anywhere, anywhere),
        scratch_shapes=[
            pltpu.VMEM((n_shard * tok, rows), jnp.bfloat16),
            pltpu.VMEM((n_shard * tok, cols), jnp.bfloat16),
            *[whole] * 6,
            dma((4,)),
            dma((n_a, n_shard - 1)),
            dma((n_a, n_shard - 1)),
            dma((n_c, n_shard - 1)),
            dma((n_c, n_shard - 1)),
            dma((n_b,)),
            dma((n_b,)),
            dma((n_b,)),
            dma((n_b,)),
        ],
        compiler_params=pltpu.CompilerParams(
            collective_id=level + 1, has_side_effects=True, vmem_limit_bytes=48 << 20
        ),
        cost_estimate=pl.CostEstimate(
            flops=2 * n_shard * tok * rows * cols, bytes_accessed=10 * rows * cols, transcendentals=0
        ),
    )(activations, cotangent, weight, momentum)


def per_device(activations, cotangent, weight, momentum, step_index):
    n_rep, n_shard = lax.axis_size("rep"), lax.axis_size("shard")
    levels = n_rep.bit_length() - 1
    branches = [functools.partial(fused, n_rep, n_shard, level) for level in range(levels)]
    averaged, momentum_new = lax.switch(
        step_index[0] % levels, branches, activations, cotangent, weight[0], momentum[0]
    )
    return averaged[None], momentum_new[None]


def solution(mesh):
    return jax.shard_map(
        per_device,
        mesh=mesh,
        in_specs=(
            P(("rep", "shard"), None),
            P(("rep", "shard"), None),
            P("rep", "shard", None),
            P("rep", "shard", None),
            P(),
        ),
        out_specs=(P("rep", "shard", None), P("rep", "shard", None)),
        check_vma=False,
    )
```

```python
import functools

import jax
import jax.numpy as jnp
from jax import lax
from jax.experimental import pallas as pl
from jax.experimental.pallas import tpu as pltpu
from jax.sharding import PartitionSpec as P

MESH = pl.DeviceIdType.MESH
STEP = 128
WINDOW = 3


def cuts(size, step):
    step = step if size % step == 0 else size
    return [(at, step) for at in range(0, size, step)]


def plan(rows, cols):
    a_chunks, c_chunks = cuts(rows, STEP), cuts(cols, STEP)
    order = sorted(
        [((i + 1) / len(c_chunks), 0, "c", i) for i in range(len(c_chunks))]
        + [((i + 1) / len(a_chunks), 1, "a", i) for i in range(len(a_chunks))]
    )
    events, rows_in, cols_in = [], 0, 0
    for _, _, kind, i in order:
        if kind == "a":
            at, size = a_chunks[i]
            block = (at, size, 0, cols_in)
            rows_in = at + size
        else:
            at, size = c_chunks[i]
            block = (0, rows_in, at, size)
            cols_in = at + size
        events.append((kind, i, at, size, block if block[1] and block[3] else None))
    return events


def kernel(
    n_rep,
    n_shard,
    by,
    act,
    cot,
    weight,
    momentum,
    avg_out,
    mom_out,
    act_all,
    cot_all,
    w_in,
    m_in,
    m_new,
    half,
    other,
    avg,
    load_sem,
    act_send,
    act_recv,
    cot_send,
    cot_recv,
    rep_send,
    rep_recv,
    mom_sem,
    avg_sem,
):
    rep, shard = lax.axis_index("rep"), lax.axis_index("shard")
    tok = cot.shape[0]
    rows, cols = weight.shape
    events = plan(rows, cols)
    ahead = lax.rem(rep + by, n_rep)
    behind = lax.rem(rep + (n_rep - by), n_rep)

    mine = pl.ds(pl.multiple_of(shard * tok, tok), tok)
    loads = [
        pltpu.make_async_copy(
            act.at[:, pl.ds(pl.multiple_of(shard * rows, rows), rows)], act_all.at[mine, :], load_sem.at[0]
        ),
        pltpu.make_async_copy(cot, cot_all.at[mine, :], load_sem.at[1]),
        pltpu.make_async_copy(momentum, m_in, load_sem.at[2]),
        pltpu.make_async_copy(weight, w_in, load_sem.at[3]),
    ]
    for load in loads:
        load.start()

    barrier = pltpu.get_barrier_semaphore()
    for off in range(1, n_shard):
        pl.semaphore_signal(
            barrier, inc=1, device_id={"shard": lax.rem(shard + off, n_shard)}, device_id_type=MESH
        )
    for partner in (ahead, behind):
        pl.semaphore_signal(barrier, inc=1, device_id={"rep": partner}, device_id_type=MESH)
    pl.semaphore_wait(barrier, n_shard + 1)

    sends = {}

    def start(kind, i, at, size, _):
        for off in range(1, n_shard):
            to = lax.rem(shard + off, n_shard)
            if kind == "a":
                copy = pltpu.make_async_remote_copy(
                    src_ref=act.at[:, pl.ds(pl.multiple_of(to * rows + at, size), size)],
                    dst_ref=act_all.at[mine, pl.ds(at, size)],
                    send_sem=act_send.at[i, off - 1],
                    recv_sem=act_recv.at[i, off - 1],
                    device_id={"shard": to},
                    device_id_type=MESH,
                )
            else:
                copy = pltpu.make_async_remote_copy(
                    src_ref=cot.at[:, pl.ds(at, size)],
                    dst_ref=cot_all.at[mine, pl.ds(at, size)],
                    send_sem=cot_send.at[i, off - 1],
                    recv_sem=cot_recv.at[i, off - 1],
                    device_id={"shard": to},
                    device_id_type=MESH,
                )
            copy.start()
            sends[kind, i, off] = copy

    for event in events[:WINDOW]:
        start(*event)

    for load in loads:
        load.wait()

    tile = STEP if rows % STEP == 0 else rows
    outs, reps, blocks = [], [], []
    for n, (kind, i, at, size, block) in enumerate(events):
        for off in range(1, n_shard):
            sends[kind, i, off].wait_recv()
        if n + WINDOW < len(events):
            start(*events[n + WINDOW])
        if block is None:
            continue
        r0, height, c0, width = block
        across = pl.ds(c0, width)

        def one(t, _):
            down = pl.ds(pl.multiple_of(r0 + t * tile, tile), tile)
            grad = lax.dot_general(
                act_all[:, down],
                cot_all[:, across],
                (((0,), (0,)), ((), ())),
                preferred_element_type=jnp.float32,
            )
            new = (0.9 * m_in[down, across].astype(jnp.float32) + grad).astype(jnp.bfloat16)
            m_new[down, across] = new
            half[down, across] = (
                w_in[down, across].astype(jnp.float32) - 0.5 * new.astype(jnp.float32)
            ).astype(jnp.bfloat16)
            return 0

        lax.fori_loop(0, height // tile, one, 0)
        e = len(blocks)
        here = (pl.ds(r0, height), across)
        copy = pltpu.make_async_remote_copy(
            src_ref=half.at[here],
            dst_ref=other.at[here],
            send_sem=rep_send.at[e],
            recv_sem=rep_recv.at[e],
            device_id={"rep": ahead},
            device_id_type=MESH,
        )
        copy.start()
        reps.append(copy)
        out = pltpu.make_async_copy(m_new.at[here], mom_out.at[here], mom_sem.at[e])
        out.start()
        outs.append(out)
        blocks.append(block)

    for e, (r0, height, c0, width) in enumerate(blocks):
        reps[e].wait_recv()
        across = pl.ds(c0, width)

        def mean(t, _):
            down = pl.ds(pl.multiple_of(r0 + t * tile, tile), tile)
            avg[down, across] = (
                0.5 * (half[down, across].astype(jnp.float32) + other[down, across].astype(jnp.float32))
            ).astype(jnp.bfloat16)
            return 0

        lax.fori_loop(0, height // tile, mean, 0)
        here = (pl.ds(r0, height), across)
        out = pltpu.make_async_copy(avg.at[here], avg_out.at[here], avg_sem.at[e])
        out.start()
        outs.append(out)

    for copy in sends.values():
        copy.wait_send()
    for copy in reps:
        copy.wait_send()
    for out in outs:
        out.wait()


def fused(n_rep, n_shard, level, activations, cotangent, weight, momentum):
    tok, (rows, cols) = cotangent.shape[0], weight.shape
    events = plan(rows, cols)
    n_a = sum(kind == "a" for kind, *_ in events)
    n_c = len(events) - n_a
    n_b = sum(event[-1] is not None for event in events)
    dma = pltpu.SemaphoreType.DMA
    whole = pltpu.VMEM((rows, cols), jnp.bfloat16)
    shape = jax.ShapeDtypeStruct((rows, cols), jnp.bfloat16)
    anywhere = pl.BlockSpec(memory_space=pl.ANY)
    return pl.pallas_call(
        functools.partial(kernel, n_rep, n_shard, 1 << level),
        out_shape=(shape, shape),
        in_specs=[anywhere] * 4,
        out_specs=(anywhere, anywhere),
        scratch_shapes=[
            pltpu.VMEM((n_shard * tok, rows), jnp.bfloat16),
            pltpu.VMEM((n_shard * tok, cols), jnp.bfloat16),
            *[whole] * 6,
            dma((4,)),
            dma((n_a, n_shard - 1)),
            dma((n_a, n_shard - 1)),
            dma((n_c, n_shard - 1)),
            dma((n_c, n_shard - 1)),
            dma((n_b,)),
            dma((n_b,)),
            dma((n_b,)),
            dma((n_b,)),
        ],
        compiler_params=pltpu.CompilerParams(
            collective_id=level + 1, has_side_effects=True, vmem_limit_bytes=48 << 20
        ),
        cost_estimate=pl.CostEstimate(
            flops=2 * n_shard * tok * rows * cols, bytes_accessed=10 * rows * cols, transcendentals=0
        ),
    )(activations, cotangent, weight, momentum)


def per_device(activations, cotangent, weight, momentum, step_index):
    n_rep, n_shard = lax.axis_size("rep"), lax.axis_size("shard")
    levels = n_rep.bit_length() - 1
    branches = [functools.partial(fused, n_rep, n_shard, level) for level in range(levels)]
    averaged, momentum_new = lax.switch(
        step_index[0] % levels, branches, activations, cotangent, weight[0], momentum[0]
    )
    return averaged[None], momentum_new[None]


def solution(mesh):
    return jax.shard_map(
        per_device,
        mesh=mesh,
        in_specs=(
            P(("rep", "shard"), None),
            P(("rep", "shard"), None),
            P("rep", "shard", None),
            P("rep", "shard", None),
            P(),
        ),
        out_specs=(P("rep", "shard", None), P("rep", "shard", None)),
        check_vma=False,
    )
```

```python
import functools

import jax
import jax.numpy as jnp
from jax import lax
from jax.experimental import pallas as pl
from jax.experimental.pallas import tpu as pltpu
from jax.sharding import PartitionSpec as P

MESH = pl.DeviceIdType.MESH
STEP = 128


def cuts(size, step):
    step = step if size % step == 0 else size
    return [(at, step) for at in range(0, size, step)]


def plan(rows, cols):
    a_chunks, c_chunks = cuts(rows, STEP), cuts(cols, STEP)
    order = sorted(
        [((i + 1) / len(c_chunks), 0, "c", i) for i in range(len(c_chunks))]
        + [((i + 1) / len(a_chunks), 1, "a", i) for i in range(len(a_chunks))]
    )
    events, rows_in, cols_in = [], 0, 0
    for _, _, kind, i in order:
        if kind == "a":
            at, size = a_chunks[i]
            block = (at, size, 0, cols_in)
            rows_in = at + size
        else:
            at, size = c_chunks[i]
            block = (0, rows_in, at, size)
            cols_in = at + size
        events.append((kind, i, at, size, block if block[1] and block[3] else None))
    return events


def kernel(
    n_rep,
    n_shard,
    by,
    act,
    cot,
    weight,
    momentum,
    avg_out,
    mom_out,
    act_all,
    cot_all,
    w_in,
    m_in,
    m_new,
    half,
    other,
    avg,
    load_sem,
    act_send,
    act_recv,
    cot_send,
    cot_recv,
    rep_send,
    rep_recv,
    mom_sem,
    avg_sem,
):
    rep, shard = lax.axis_index("rep"), lax.axis_index("shard")
    tok = cot.shape[0]
    rows, cols = weight.shape
    events = plan(rows, cols)
    ahead = lax.rem(rep + by, n_rep)
    behind = lax.rem(rep + (n_rep - by), n_rep)

    mine = pl.ds(pl.multiple_of(shard * tok, tok), tok)
    loads = [
        pltpu.make_async_copy(
            act.at[:, pl.ds(pl.multiple_of(shard * rows, rows), rows)], act_all.at[mine, :], load_sem.at[0]
        ),
        pltpu.make_async_copy(cot, cot_all.at[mine, :], load_sem.at[1]),
        pltpu.make_async_copy(momentum, m_in, load_sem.at[2]),
        pltpu.make_async_copy(weight, w_in, load_sem.at[3]),
    ]
    for load in loads:
        load.start()

    barrier = pltpu.get_barrier_semaphore()
    for off in range(1, n_shard):
        pl.semaphore_signal(
            barrier, inc=1, device_id={"shard": lax.rem(shard + off, n_shard)}, device_id_type=MESH
        )
    for partner in (ahead, behind):
        pl.semaphore_signal(barrier, inc=1, device_id={"rep": partner}, device_id_type=MESH)
    pl.semaphore_wait(barrier, n_shard + 1)

    sends = {}

    def start(kind, i, at, size, _):
        if kind == "c":
            relay(i, at, size, 0)
            return
        for off in range(1, n_shard):
            to = lax.rem(shard + off, n_shard)
            copy = pltpu.make_async_remote_copy(
                src_ref=act.at[:, pl.ds(pl.multiple_of(to * rows + at, size), size)],
                dst_ref=act_all.at[mine, pl.ds(at, size)],
                send_sem=act_send.at[i, off - 1],
                recv_sem=act_recv.at[i, off - 1],
                device_id={"shard": to},
                device_id_type=MESH,
            )
            copy.start()
            sends[i, off] = copy

    def hop(i, at, size, side, far, come):
        way = 1 - 2 * side
        owner = shard - way * (far + come)
        slot = cot_all.at[pl.ds(pl.multiple_of(owner * tok, tok), tok), pl.ds(at, size)]
        return pltpu.make_async_remote_copy(
            src_ref=slot if far or come else cot.at[:, pl.ds(at, size)],
            dst_ref=slot,
            send_sem=cot_send.at[i, side, far],
            recv_sem=cot_recv.at[i, side, far],
            device_id={"shard": shard - way if come else shard + way},
            device_id_type=MESH,
        )

    def passes(side, far):
        if side == 0:
            return (shard >= far) & (shard + 1 < n_shard)
        return (shard + far < n_shard) & (shard >= 1)

    def comes(side, far):
        return shard >= far + 1 if side == 0 else shard + far + 1 < n_shard

    def relay(i, at, size, far):
        for side in range(2):
            if far:
                pl.when(comes(side, far - 1))(lambda side=side: hop(i, at, size, side, far - 1, 1).wait_recv())
            if far < last:
                pl.when(passes(side, far))(lambda side=side: hop(i, at, size, side, far, 0).start())

    last = n_shard - 1

    def turn(n):
        if 0 <= n + last < len(events):
            start(*events[n + last])
        for far in range(1, last):
            if 0 <= n + last - far < len(events):
                kind, i, at, size, _ = events[n + last - far]
                if kind == "c":
                    relay(i, at, size, far)

    for n in range(-last, 0):
        turn(n)

    for load in loads:
        load.wait()

    tile = STEP if rows % STEP == 0 else rows
    outs, reps, blocks = [], [], []
    for n, (kind, i, at, size, block) in enumerate(events):
        if kind == "c":
            relay(i, at, size, last)
        else:
            for off in range(1, n_shard):
                sends[i, off].wait_recv()
        turn(n)
        if block is None:
            continue
        r0, height, c0, width = block
        across = pl.ds(c0, width)

        def one(t, _):
            down = pl.ds(pl.multiple_of(r0 + t * tile, tile), tile)
            grad = lax.dot_general(
                act_all[:, down],
                cot_all[:, across],
                (((0,), (0,)), ((), ())),
                preferred_element_type=jnp.float32,
            )
            new = (0.9 * m_in[down, across].astype(jnp.float32) + grad).astype(jnp.bfloat16)
            m_new[down, across] = new
            half[down, across] = (
                w_in[down, across].astype(jnp.float32) - 0.5 * new.astype(jnp.float32)
            ).astype(jnp.bfloat16)
            return 0

        lax.fori_loop(0, height // tile, one, 0)
        e = len(blocks)
        here = (pl.ds(r0, height), across)
        copy = pltpu.make_async_remote_copy(
            src_ref=half.at[here],
            dst_ref=other.at[here],
            send_sem=rep_send.at[e],
            recv_sem=rep_recv.at[e],
            device_id={"rep": ahead},
            device_id_type=MESH,
        )
        copy.start()
        reps.append(copy)
        out = pltpu.make_async_copy(m_new.at[here], mom_out.at[here], mom_sem.at[e])
        out.start()
        outs.append(out)
        blocks.append(block)

    for e, (r0, height, c0, width) in enumerate(blocks):
        reps[e].wait_recv()
        across = pl.ds(c0, width)

        def mean(t, _):
            down = pl.ds(pl.multiple_of(r0 + t * tile, tile), tile)
            avg[down, across] = (
                0.5 * (half[down, across].astype(jnp.float32) + other[down, across].astype(jnp.float32))
            ).astype(jnp.bfloat16)
            return 0

        lax.fori_loop(0, height // tile, mean, 0)
        here = (pl.ds(r0, height), across)
        out = pltpu.make_async_copy(avg.at[here], avg_out.at[here], avg_sem.at[e])
        out.start()
        outs.append(out)

    for copy in sends.values():
        copy.wait_send()
    for kind, i, at, size, _ in events:
        if kind == "c":
            for far in range(last):
                for side in range(2):
                    pl.when(passes(side, far))(
                        lambda i=i, at=at, size=size, side=side, far=far: hop(i, at, size, side, far, 0).wait_send()
                    )
    for copy in reps:
        copy.wait_send()
    for out in outs:
        out.wait()


def fused(n_rep, n_shard, level, activations, cotangent, weight, momentum):
    tok, (rows, cols) = cotangent.shape[0], weight.shape
    events = plan(rows, cols)
    n_a = sum(kind == "a" for kind, *_ in events)
    n_c = len(events) - n_a
    n_b = sum(event[-1] is not None for event in events)
    dma = pltpu.SemaphoreType.DMA
    whole = pltpu.VMEM((rows, cols), jnp.bfloat16)
    shape = jax.ShapeDtypeStruct((rows, cols), jnp.bfloat16)
    anywhere = pl.BlockSpec(memory_space=pl.ANY)
    return pl.pallas_call(
        functools.partial(kernel, n_rep, n_shard, 1 << level),
        out_shape=(shape, shape),
        in_specs=[anywhere] * 4,
        out_specs=(anywhere, anywhere),
        scratch_shapes=[
            pltpu.VMEM((n_shard * tok, rows), jnp.bfloat16),
            pltpu.VMEM((n_shard * tok, cols), jnp.bfloat16),
            *[whole] * 6,
            dma((4,)),
            dma((n_a, n_shard - 1)),
            dma((n_a, n_shard - 1)),
            dma((n_c, 2, n_shard - 1)),
            dma((n_c, 2, n_shard - 1)),
            dma((n_b,)),
            dma((n_b,)),
            dma((n_b,)),
            dma((n_b,)),
        ],
        compiler_params=pltpu.CompilerParams(
            collective_id=level + 1, has_side_effects=True, vmem_limit_bytes=48 << 20
        ),
        cost_estimate=pl.CostEstimate(
            flops=2 * n_shard * tok * rows * cols, bytes_accessed=10 * rows * cols, transcendentals=0
        ),
    )(activations, cotangent, weight, momentum)


def per_device(activations, cotangent, weight, momentum, step_index):
    n_rep, n_shard = lax.axis_size("rep"), lax.axis_size("shard")
    levels = n_rep.bit_length() - 1
    branches = [functools.partial(fused, n_rep, n_shard, level) for level in range(levels)]
    averaged, momentum_new = lax.switch(
        step_index[0] % levels, branches, activations, cotangent, weight[0], momentum[0]
    )
    return averaged[None], momentum_new[None]


def solution(mesh):
    return jax.shard_map(
        per_device,
        mesh=mesh,
        in_specs=(
            P(("rep", "shard"), None),
            P(("rep", "shard"), None),
            P("rep", "shard", None),
            P("rep", "shard", None),
            P(),
        ),
        out_specs=(P("rep", "shard", None), P("rep", "shard", None)),
        check_vma=False,
    )
```

```python
import functools
import math

import jax
import jax.numpy as jnp
from jax import lax
from jax.experimental import pallas as pl
from jax.experimental.pallas import tpu as pltpu
from jax.sharding import PartitionSpec as P

MESH = pl.DeviceIdType.MESH
STEP = 128


def cuts(size, step=STEP):
    if size % step:
        return [(0, size)]
    chunks, at = [(0, step)], step
    while at < size:
        width = min(2 * step, size - at)
        chunks.append((at, width))
        at += width
    return chunks


def tiles(block, step=2 * STEP):
    r0, height, c0, width = block
    return [
        (pl.ds(r, min(step, r0 + height - r)), pl.ds(c, min(step, c0 + width - c)))
        for r in range(r0, r0 + height, step)
        for c in range(c0, c0 + width, step)
    ]


def plan(rows, cols):
    a_chunks, c_chunks = cuts(rows), cuts(cols)
    order = sorted(
        [((at + size) / cols, 0, "c", i) for i, (at, size) in enumerate(c_chunks)]
        + [((at + size) / rows, 1, "a", i) for i, (at, size) in enumerate(a_chunks)]
    )
    events, rows_in, cols_in = [], 0, 0
    for _, _, kind, i in order:
        if kind == "a":
            at, size = a_chunks[i]
            block = (at, size, 0, cols_in)
            rows_in = at + size
        else:
            at, size = c_chunks[i]
            block = (0, rows_in, at, size)
            cols_in = at + size
        events.append((kind, i, at, size, block if block[1] and block[3] else None))
    return events


def kernel(
    n_rep,
    n_shard,
    by,
    act,
    cot,
    weight,
    momentum,
    avg_out,
    mom_out,
    act_all,
    act_t,
    cot_all,
    w_in,
    m_in,
    m_new,
    half,
    other,
    avg,
    load_sem,
    act_send,
    act_recv,
    cot_send,
    cot_recv,
    rep_send,
    rep_recv,
    mom_sem,
    avg_sem,
):
    rep, shard = lax.axis_index("rep"), lax.axis_index("shard")
    tok = cot.shape[0]
    rows, cols = weight.shape
    events = plan(rows, cols)
    ahead = lax.rem(rep + by, n_rep)
    behind = lax.rem(rep + (n_rep - by), n_rep)

    mine = pl.ds(pl.multiple_of(shard * tok, tok), tok)
    loads = [
        pltpu.make_async_copy(
            act.at[:, pl.ds(pl.multiple_of(shard * rows, rows), rows)], act_all.at[mine, :], load_sem.at[0]
        ),
        pltpu.make_async_copy(cot, cot_all.at[mine, :], load_sem.at[1]),
        pltpu.make_async_copy(momentum, m_in, load_sem.at[2]),
        pltpu.make_async_copy(weight, w_in, load_sem.at[3]),
    ]
    for load in loads:
        load.start()

    barrier = pltpu.get_barrier_semaphore()
    for off in range(1, n_shard):
        pl.semaphore_signal(
            barrier, inc=1, device_id={"shard": lax.rem(shard + off, n_shard)}, device_id_type=MESH
        )
    for partner in (ahead, behind):
        pl.semaphore_signal(barrier, inc=1, device_id={"rep": partner}, device_id_type=MESH)
    pl.semaphore_wait(barrier, n_shard + 1)

    sends = {}

    def start(kind, i, at, size, _):
        if kind == "c":
            relay(i, at, size, 0)
            return
        for off in range(1, n_shard):
            to = lax.rem(shard + off, n_shard)
            copy = pltpu.make_async_remote_copy(
                src_ref=act.at[:, pl.ds(pl.multiple_of(to * rows + at, math.gcd(rows, at)), size)],
                dst_ref=act_all.at[mine, pl.ds(at, size)],
                send_sem=act_send.at[i, off - 1],
                recv_sem=act_recv.at[i, off - 1],
                device_id={"shard": to},
                device_id_type=MESH,
            )
            copy.start()
            sends[i, off] = copy

    def hop(i, at, size, side, far, come):
        way = 1 - 2 * side
        owner = shard - way * (far + come)
        slot = cot_all.at[pl.ds(pl.multiple_of(owner * tok, tok), tok), pl.ds(at, size)]
        return pltpu.make_async_remote_copy(
            src_ref=slot if far or come else cot.at[:, pl.ds(at, size)],
            dst_ref=slot,
            send_sem=cot_send.at[i, side, far],
            recv_sem=cot_recv.at[i, side, far],
            device_id={"shard": shard - way if come else shard + way},
            device_id_type=MESH,
        )

    def passes(side, far):
        if side == 0:
            return (shard >= far) & (shard + 1 < n_shard)
        return (shard + far < n_shard) & (shard >= 1)

    def comes(side, far):
        return shard >= far + 1 if side == 0 else shard + far + 1 < n_shard

    def relay(i, at, size, far):
        for side in range(2):
            if far:
                pl.when(comes(side, far - 1))(lambda side=side: hop(i, at, size, side, far - 1, 1).wait_recv())
            if far < last:
                pl.when(passes(side, far))(lambda side=side: hop(i, at, size, side, far, 0).start())

    last = n_shard - 1

    def turn(n):
        if 0 <= n + last < len(events):
            start(*events[n + last])
        for far in range(1, last):
            if 0 <= n + last - far < len(events):
                kind, i, at, size, _ = events[n + last - far]
                if kind == "c":
                    relay(i, at, size, far)

    for n in range(-last, 0):
        turn(n)

    for load in loads:
        load.wait()

    outs, reps, blocks = [], [], []
    for n, (kind, i, at, size, block) in enumerate(events):
        if kind == "c":
            relay(i, at, size, last)
        else:
            for off in range(1, n_shard):
                sends[i, off].wait_recv()
        turn(n)
        if kind == "a":
            act_t[pl.ds(at, size), :] = act_all[:, pl.ds(at, size)].T
        if block is None:
            continue
        r0, height, c0, width = block
        for tile in tiles(block):
            grad = jnp.dot(act_t[tile[0], :], cot_all[:, tile[1]], preferred_element_type=jnp.float32)
            new = (0.9 * m_in[tile].astype(jnp.float32) + grad).astype(jnp.bfloat16)
            m_new[tile] = new
            half[tile] = (w_in[tile].astype(jnp.float32) - 0.5 * new.astype(jnp.float32)).astype(jnp.bfloat16)
        e = len(blocks)
        here = (pl.ds(r0, height), pl.ds(c0, width))
        copy = pltpu.make_async_remote_copy(
            src_ref=half.at[here],
            dst_ref=other.at[here],
            send_sem=rep_send.at[e],
            recv_sem=rep_recv.at[e],
            device_id={"rep": ahead},
            device_id_type=MESH,
        )
        copy.start()
        reps.append(copy)
        out = pltpu.make_async_copy(m_new.at[here], mom_out.at[here], mom_sem.at[e])
        out.start()
        outs.append(out)
        blocks.append(block)

    for e, block in enumerate(blocks):
        r0, height, c0, width = block
        reps[e].wait_recv()
        for tile in tiles(block):
            avg[tile] = (0.5 * (half[tile].astype(jnp.float32) + other[tile].astype(jnp.float32))).astype(jnp.bfloat16)
        here = (pl.ds(r0, height), pl.ds(c0, width))
        out = pltpu.make_async_copy(avg.at[here], avg_out.at[here], avg_sem.at[e])
        out.start()
        outs.append(out)

    for copy in sends.values():
        copy.wait_send()
    for kind, i, at, size, _ in events:
        if kind == "c":
            for far in range(last):
                for side in range(2):
                    pl.when(passes(side, far))(
                        lambda i=i, at=at, size=size, side=side, far=far: hop(i, at, size, side, far, 0).wait_send()
                    )
    for copy in reps:
        copy.wait_send()
    for out in outs:
        out.wait()


def fused(n_rep, n_shard, level, activations, cotangent, weight, momentum):
    tok, (rows, cols) = cotangent.shape[0], weight.shape
    events = plan(rows, cols)
    n_a = sum(kind == "a" for kind, *_ in events)
    n_c = len(events) - n_a
    n_b = sum(event[-1] is not None for event in events)
    dma = pltpu.SemaphoreType.DMA
    whole = pltpu.VMEM((rows, cols), jnp.bfloat16)
    shape = jax.ShapeDtypeStruct((rows, cols), jnp.bfloat16)
    anywhere = pl.BlockSpec(memory_space=pl.ANY)
    return pl.pallas_call(
        functools.partial(kernel, n_rep, n_shard, 1 << level),
        out_shape=(shape, shape),
        in_specs=[anywhere] * 4,
        out_specs=(anywhere, anywhere),
        scratch_shapes=[
            pltpu.VMEM((n_shard * tok, rows), jnp.bfloat16),
            pltpu.VMEM((rows, n_shard * tok), jnp.bfloat16),
            pltpu.VMEM((n_shard * tok, cols), jnp.bfloat16),
            *[whole] * 6,
            dma((4,)),
            dma((n_a, n_shard - 1)),
            dma((n_a, n_shard - 1)),
            dma((n_c, 2, n_shard - 1)),
            dma((n_c, 2, n_shard - 1)),
            dma((n_b,)),
            dma((n_b,)),
            dma((n_b,)),
            dma((n_b,)),
        ],
        compiler_params=pltpu.CompilerParams(
            collective_id=level + 1, has_side_effects=True, vmem_limit_bytes=48 << 20
        ),
        cost_estimate=pl.CostEstimate(
            flops=2 * n_shard * tok * rows * cols, bytes_accessed=10 * rows * cols, transcendentals=0
        ),
    )(activations, cotangent, weight, momentum)


def per_device(activations, cotangent, weight, momentum, step_index):
    n_rep, n_shard = lax.axis_size("rep"), lax.axis_size("shard")
    levels = n_rep.bit_length() - 1
    branches = [functools.partial(fused, n_rep, n_shard, level) for level in range(levels)]
    averaged, momentum_new = lax.switch(
        step_index[0] % levels, branches, activations, cotangent, weight[0], momentum[0]
    )
    return averaged[None], momentum_new[None]


def solution(mesh):
    return jax.shard_map(
        per_device,
        mesh=mesh,
        in_specs=(
            P(("rep", "shard"), None),
            P(("rep", "shard"), None),
            P("rep", "shard", None),
            P("rep", "shard", None),
            P(),
        ),
        out_specs=(P("rep", "shard", None), P("rep", "shard", None)),
        check_vma=False,
    )
```

```python
import functools
import math

import jax
import jax.numpy as jnp
from jax import lax
from jax.experimental import pallas as pl
from jax.experimental.pallas import tpu as pltpu
from jax.sharding import PartitionSpec as P

MESH = pl.DeviceIdType.MESH
STEP = 128


def cuts(size, step=STEP):
    if size % step:
        return [(0, size)]
    chunks, at = [(0, step)], step
    while at < size:
        width = min(2 * step, size - at)
        chunks.append((at, width))
        at += width
    return chunks


def tiles(block, step=2 * STEP):
    r0, height, c0, width = block
    return [
        (pl.ds(r, min(step, r0 + height - r)), pl.ds(c, min(step, c0 + width - c)))
        for r in range(r0, r0 + height, step)
        for c in range(c0, c0 + width, step)
    ]


def plan(rows, cols):
    a_chunks, c_chunks = cuts(rows), cuts(cols)
    order = sorted(
        [((at + size) / cols, 0, "c", i) for i, (at, size) in enumerate(c_chunks)]
        + [((at + size) / rows, 1, "a", i) for i, (at, size) in enumerate(a_chunks)]
    )
    events, rows_in, cols_in = [], 0, 0
    for _, _, kind, i in order:
        if kind == "a":
            at, size = a_chunks[i]
            block = (at, size, 0, cols_in)
            rows_in = at + size
        else:
            at, size = c_chunks[i]
            block = (0, rows_in, at, size)
            cols_in = at + size
        events.append((kind, i, at, size, block if block[1] and block[3] else None))
    return events


def kernel(
    n_rep,
    n_shard,
    by,
    act,
    cot,
    weight,
    momentum,
    avg_out,
    mom_out,
    act_all,
    act_t,
    cot_all,
    w_in,
    m_in,
    m_new,
    half,
    other,
    avg,
    load_sem,
    act_send,
    act_recv,
    cot_send,
    cot_recv,
    rep_send,
    rep_recv,
    mom_sem,
    avg_sem,
):
    rep, shard = lax.axis_index("rep"), lax.axis_index("shard")
    tok = cot.shape[0]
    rows, cols = weight.shape
    events = plan(rows, cols)
    ahead = lax.rem(rep + by, n_rep)
    behind = lax.rem(rep + (n_rep - by), n_rep)

    mine = pl.ds(pl.multiple_of(shard * tok, tok), tok)
    loads = [
        pltpu.make_async_copy(
            act.at[:, pl.ds(pl.multiple_of(shard * rows, rows), rows)], act_all.at[mine, :], load_sem.at[0]
        ),
        pltpu.make_async_copy(cot, cot_all.at[mine, :], load_sem.at[1]),
        pltpu.make_async_copy(momentum, m_in, load_sem.at[2]),
        pltpu.make_async_copy(weight, w_in, load_sem.at[3]),
    ]
    for load in loads:
        load.start()

    barrier = pltpu.get_barrier_semaphore()
    for off in range(1, n_shard):
        pl.semaphore_signal(
            barrier, inc=1, device_id={"shard": lax.rem(shard + off, n_shard)}, device_id_type=MESH
        )
    for partner in (ahead, behind):
        pl.semaphore_signal(barrier, inc=1, device_id={"rep": partner}, device_id_type=MESH)
    pl.semaphore_wait(barrier, n_shard + 1)

    sends = {}

    def start(kind, i, at, size, _):
        for off in range(1, n_shard):
            to = lax.rem(shard + off, n_shard)
            copy = pltpu.make_async_remote_copy(
                src_ref=act.at[:, pl.ds(pl.multiple_of(to * rows + at, math.gcd(rows, at)), size)],
                dst_ref=act_all.at[mine, pl.ds(at, size)],
                send_sem=act_send.at[i, off - 1],
                recv_sem=act_recv.at[i, off - 1],
                device_id={"shard": to},
                device_id_type=MESH,
            )
            copy.start()
            sends[i, off] = copy

    def hop(i, at, size, side, far, come):
        way = 1 - 2 * side
        owner = shard - way * (far + come)
        slot = cot_all.at[pl.ds(pl.multiple_of(owner * tok, tok), tok), pl.ds(at, size)]
        return pltpu.make_async_remote_copy(
            src_ref=slot if far or come else cot.at[:, pl.ds(at, size)],
            dst_ref=slot,
            send_sem=cot_send.at[i, side, far],
            recv_sem=cot_recv.at[i, side, far],
            device_id={"shard": shard - way if come else shard + way},
            device_id_type=MESH,
        )

    def passes(side, far):
        if side == 0:
            return (shard >= far) & (shard + 1 < n_shard)
        return (shard + far < n_shard) & (shard >= 1)

    def comes(side, far):
        return shard >= far + 1 if side == 0 else shard + far + 1 < n_shard

    def relay(i, at, size, far):
        for side in range(2):
            if far:
                pl.when(comes(side, far - 1))(lambda side=side: hop(i, at, size, side, far - 1, 1).wait_recv())
            if far < last:
                pl.when(passes(side, far))(lambda side=side: hop(i, at, size, side, far, 0).start())

    last = n_shard - 1

    def turn(n):
        for later, (kind, i, at, size, _) in enumerate(events):
            if kind == "a":
                if later - n == last + 1:
                    start(kind, i, at, size, _)
            elif (later - n) % 2 == 0 and 0 < later - n <= 2 * last:
                relay(i, at, size, last - (later - n) // 2)

    for n in range(-2 * last, 0):
        turn(n)

    for load in loads:
        load.wait()

    outs, reps, blocks = [], [], []
    for n, (kind, i, at, size, block) in enumerate(events):
        if kind == "c":
            relay(i, at, size, last)
        else:
            for off in range(1, n_shard):
                sends[i, off].wait_recv()
        turn(n)
        if kind == "a":
            act_t[pl.ds(at, size), :] = act_all[:, pl.ds(at, size)].T
        if block is None:
            continue
        r0, height, c0, width = block
        for tile in tiles(block):
            grad = jnp.dot(act_t[tile[0], :], cot_all[:, tile[1]], preferred_element_type=jnp.float32)
            new = (0.9 * m_in[tile].astype(jnp.float32) + grad).astype(jnp.bfloat16)
            m_new[tile] = new
            half[tile] = (w_in[tile].astype(jnp.float32) - 0.5 * new.astype(jnp.float32)).astype(jnp.bfloat16)
        e = len(blocks)
        here = (pl.ds(r0, height), pl.ds(c0, width))
        copy = pltpu.make_async_remote_copy(
            src_ref=half.at[here],
            dst_ref=other.at[here],
            send_sem=rep_send.at[e],
            recv_sem=rep_recv.at[e],
            device_id={"rep": ahead},
            device_id_type=MESH,
        )
        copy.start()
        reps.append(copy)
        out = pltpu.make_async_copy(m_new.at[here], mom_out.at[here], mom_sem.at[e])
        out.start()
        outs.append(out)
        blocks.append(block)

    for e, block in enumerate(blocks):
        r0, height, c0, width = block
        reps[e].wait_recv()
        for tile in tiles(block):
            avg[tile] = (0.5 * (half[tile].astype(jnp.float32) + other[tile].astype(jnp.float32))).astype(jnp.bfloat16)
        here = (pl.ds(r0, height), pl.ds(c0, width))
        out = pltpu.make_async_copy(avg.at[here], avg_out.at[here], avg_sem.at[e])
        out.start()
        outs.append(out)

    for copy in sends.values():
        copy.wait_send()
    for kind, i, at, size, _ in events:
        if kind == "c":
            for far in range(last):
                for side in range(2):
                    pl.when(passes(side, far))(
                        lambda i=i, at=at, size=size, side=side, far=far: hop(i, at, size, side, far, 0).wait_send()
                    )
    for copy in reps:
        copy.wait_send()
    for out in outs:
        out.wait()


def fused(n_rep, n_shard, level, activations, cotangent, weight, momentum):
    tok, (rows, cols) = cotangent.shape[0], weight.shape
    events = plan(rows, cols)
    n_a = sum(kind == "a" for kind, *_ in events)
    n_c = len(events) - n_a
    n_b = sum(event[-1] is not None for event in events)
    dma = pltpu.SemaphoreType.DMA
    whole = pltpu.VMEM((rows, cols), jnp.bfloat16)
    shape = jax.ShapeDtypeStruct((rows, cols), jnp.bfloat16)
    anywhere = pl.BlockSpec(memory_space=pl.ANY)
    return pl.pallas_call(
        functools.partial(kernel, n_rep, n_shard, 1 << level),
        out_shape=(shape, shape),
        in_specs=[anywhere] * 4,
        out_specs=(anywhere, anywhere),
        scratch_shapes=[
            pltpu.VMEM((n_shard * tok, rows), jnp.bfloat16),
            pltpu.VMEM((rows, n_shard * tok), jnp.bfloat16),
            pltpu.VMEM((n_shard * tok, cols), jnp.bfloat16),
            *[whole] * 6,
            dma((4,)),
            dma((n_a, n_shard - 1)),
            dma((n_a, n_shard - 1)),
            dma((n_c, 2, n_shard - 1)),
            dma((n_c, 2, n_shard - 1)),
            dma((n_b,)),
            dma((n_b,)),
            dma((n_b,)),
            dma((n_b,)),
        ],
        compiler_params=pltpu.CompilerParams(
            collective_id=level + 1, has_side_effects=True, vmem_limit_bytes=48 << 20
        ),
        cost_estimate=pl.CostEstimate(
            flops=2 * n_shard * tok * rows * cols, bytes_accessed=10 * rows * cols, transcendentals=0
        ),
    )(activations, cotangent, weight, momentum)


def per_device(activations, cotangent, weight, momentum, step_index):
    n_rep, n_shard = lax.axis_size("rep"), lax.axis_size("shard")
    levels = n_rep.bit_length() - 1
    branches = [functools.partial(fused, n_rep, n_shard, level) for level in range(levels)]
    averaged, momentum_new = lax.switch(
        step_index[0] % levels, branches, activations, cotangent, weight[0], momentum[0]
    )
    return averaged[None], momentum_new[None]


def solution(mesh):
    return jax.shard_map(
        per_device,
        mesh=mesh,
        in_specs=(
            P(("rep", "shard"), None),
            P(("rep", "shard"), None),
            P("rep", "shard", None),
            P("rep", "shard", None),
            P(),
        ),
        out_specs=(P("rep", "shard", None), P("rep", "shard", None)),
        check_vma=False,
    )
```

```python
import functools
import math

import jax
import jax.numpy as jnp
from jax import lax
from jax.experimental import pallas as pl
from jax.experimental.pallas import tpu as pltpu
from jax.sharding import PartitionSpec as P

MESH = pl.DeviceIdType.MESH
STEP = 128
WINDOW = 2


def cuts(size, step=STEP):
    if size % step:
        return [(0, size)]
    chunks, at = [(0, step)], step
    while at < size:
        width = min(2 * step, size - at)
        chunks.append((at, width))
        at += width
    return chunks


def tiles(block, step=2 * STEP):
    r0, height, c0, width = block
    return [
        (pl.ds(r, min(step, r0 + height - r)), pl.ds(c, min(step, c0 + width - c)))
        for r in range(r0, r0 + height, step)
        for c in range(c0, c0 + width, step)
    ]


def plan(rows, cols):
    a_chunks, c_chunks = cuts(rows), cuts(cols)
    order = sorted(
        [((at + size) / cols, 0, "c", i) for i, (at, size) in enumerate(c_chunks)]
        + [((at + size) / rows, 1, "a", i) for i, (at, size) in enumerate(a_chunks)]
    )
    events, rows_in, cols_in = [], 0, 0
    for _, _, kind, i in order:
        if kind == "a":
            at, size = a_chunks[i]
            block = (at, size, 0, cols_in)
            rows_in = at + size
        else:
            at, size = c_chunks[i]
            block = (0, rows_in, at, size)
            cols_in = at + size
        events.append((kind, i, at, size, block if block[1] and block[3] else None))
    return events


def kernel(
    n_rep,
    n_shard,
    by,
    act,
    cot,
    weight,
    momentum,
    avg_out,
    mom_out,
    act_all,
    act_t,
    cot_all,
    w_in,
    m_in,
    m_new,
    half,
    other,
    avg,
    load_sem,
    act_send,
    act_recv,
    cot_send,
    cot_recv,
    rep_send,
    rep_recv,
    mom_sem,
    avg_sem,
):
    rep, shard = lax.axis_index("rep"), lax.axis_index("shard")
    tok = cot.shape[0]
    rows, cols = weight.shape
    events = plan(rows, cols)
    ahead = lax.rem(rep + by, n_rep)
    behind = lax.rem(rep + (n_rep - by), n_rep)

    mine = pl.ds(pl.multiple_of(shard * tok, tok), tok)
    loads = [
        pltpu.make_async_copy(
            act.at[:, pl.ds(pl.multiple_of(shard * rows, rows), rows)], act_all.at[mine, :], load_sem.at[0]
        ),
        pltpu.make_async_copy(cot, cot_all.at[mine, :], load_sem.at[1]),
        pltpu.make_async_copy(momentum, m_in, load_sem.at[2]),
        pltpu.make_async_copy(weight, w_in, load_sem.at[3]),
    ]
    for load in loads:
        load.start()

    barrier = pltpu.get_barrier_semaphore()
    for off in range(1, n_shard):
        pl.semaphore_signal(
            barrier, inc=1, device_id={"shard": lax.rem(shard + off, n_shard)}, device_id_type=MESH
        )
    for partner in (ahead, behind):
        pl.semaphore_signal(barrier, inc=1, device_id={"rep": partner}, device_id_type=MESH)
    pl.semaphore_wait(barrier, n_shard + 1)

    sends = {}

    def start(kind, i, at, size, _):
        for off in range(1, n_shard):
            to = lax.rem(shard + off, n_shard)
            if kind == "a":
                copy = pltpu.make_async_remote_copy(
                    src_ref=act.at[:, pl.ds(pl.multiple_of(to * rows + at, math.gcd(rows, at)), size)],
                    dst_ref=act_all.at[mine, pl.ds(at, size)],
                    send_sem=act_send.at[i, off - 1],
                    recv_sem=act_recv.at[i, off - 1],
                    device_id={"shard": to},
                    device_id_type=MESH,
                )
            else:
                copy = pltpu.make_async_remote_copy(
                    src_ref=cot.at[:, pl.ds(at, size)],
                    dst_ref=cot_all.at[mine, pl.ds(at, size)],
                    send_sem=cot_send.at[i, off - 1],
                    recv_sem=cot_recv.at[i, off - 1],
                    device_id={"shard": to},
                    device_id_type=MESH,
                )
            copy.start()
            sends[kind, i, off] = copy

    for event in events[:WINDOW]:
        start(*event)

    for load in loads:
        load.wait()

    outs, reps, blocks = [], [], []
    for n, (kind, i, at, size, block) in enumerate(events):
        for off in range(1, n_shard):
            sends[kind, i, off].wait_recv()
        if n + WINDOW < len(events):
            start(*events[n + WINDOW])
        if kind == "a":
            act_t[pl.ds(at, size), :] = act_all[:, pl.ds(at, size)].T
        if block is None:
            continue
        r0, height, c0, width = block
        for tile in tiles(block):
            grad = jnp.dot(act_t[tile[0], :], cot_all[:, tile[1]], preferred_element_type=jnp.float32)
            new = (0.9 * m_in[tile].astype(jnp.float32) + grad).astype(jnp.bfloat16)
            m_new[tile] = new
            half[tile] = (w_in[tile].astype(jnp.float32) - 0.5 * new.astype(jnp.float32)).astype(jnp.bfloat16)
        e = len(blocks)
        here = (pl.ds(r0, height), pl.ds(c0, width))
        copy = pltpu.make_async_remote_copy(
            src_ref=half.at[here],
            dst_ref=other.at[here],
            send_sem=rep_send.at[e],
            recv_sem=rep_recv.at[e],
            device_id={"rep": ahead},
            device_id_type=MESH,
        )
        copy.start()
        reps.append(copy)
        out = pltpu.make_async_copy(m_new.at[here], mom_out.at[here], mom_sem.at[e])
        out.start()
        outs.append(out)
        blocks.append(block)

    for e, block in enumerate(blocks):
        r0, height, c0, width = block
        reps[e].wait_recv()
        for tile in tiles(block):
            avg[tile] = (0.5 * (half[tile].astype(jnp.float32) + other[tile].astype(jnp.float32))).astype(jnp.bfloat16)
        here = (pl.ds(r0, height), pl.ds(c0, width))
        out = pltpu.make_async_copy(avg.at[here], avg_out.at[here], avg_sem.at[e])
        out.start()
        outs.append(out)

    for copy in sends.values():
        copy.wait_send()
    for copy in reps:
        copy.wait_send()
    for out in outs:
        out.wait()


def fused(n_rep, n_shard, level, activations, cotangent, weight, momentum):
    tok, (rows, cols) = cotangent.shape[0], weight.shape
    events = plan(rows, cols)
    n_a = sum(kind == "a" for kind, *_ in events)
    n_c = len(events) - n_a
    n_b = sum(event[-1] is not None for event in events)
    dma = pltpu.SemaphoreType.DMA
    whole = pltpu.VMEM((rows, cols), jnp.bfloat16)
    shape = jax.ShapeDtypeStruct((rows, cols), jnp.bfloat16)
    anywhere = pl.BlockSpec(memory_space=pl.ANY)
    return pl.pallas_call(
        functools.partial(kernel, n_rep, n_shard, 1 << level),
        out_shape=(shape, shape),
        in_specs=[anywhere] * 4,
        out_specs=(anywhere, anywhere),
        scratch_shapes=[
            pltpu.VMEM((n_shard * tok, rows), jnp.bfloat16),
            pltpu.VMEM((rows, n_shard * tok), jnp.bfloat16),
            pltpu.VMEM((n_shard * tok, cols), jnp.bfloat16),
            *[whole] * 6,
            dma((4,)),
            dma((n_a, n_shard - 1)),
            dma((n_a, n_shard - 1)),
            dma((n_c, n_shard - 1)),
            dma((n_c, n_shard - 1)),
            dma((n_b,)),
            dma((n_b,)),
            dma((n_b,)),
            dma((n_b,)),
        ],
        compiler_params=pltpu.CompilerParams(
            collective_id=level + 1, has_side_effects=True, vmem_limit_bytes=48 << 20
        ),
        cost_estimate=pl.CostEstimate(
            flops=2 * n_shard * tok * rows * cols, bytes_accessed=10 * rows * cols, transcendentals=0
        ),
    )(activations, cotangent, weight, momentum)


def per_device(activations, cotangent, weight, momentum, step_index):
    n_rep, n_shard = lax.axis_size("rep"), lax.axis_size("shard")
    levels = n_rep.bit_length() - 1
    branches = [functools.partial(fused, n_rep, n_shard, level) for level in range(levels)]
    averaged, momentum_new = lax.switch(
        step_index[0] % levels, branches, activations, cotangent, weight[0], momentum[0]
    )
    return averaged[None], momentum_new[None]


def solution(mesh):
    return jax.shard_map(
        per_device,
        mesh=mesh,
        in_specs=(
            P(("rep", "shard"), None),
            P(("rep", "shard"), None),
            P("rep", "shard", None),
            P("rep", "shard", None),
            P(),
        ),
        out_specs=(P("rep", "shard", None), P("rep", "shard", None)),
        check_vma=False,
    )
```
